512 devices in a mesh: dp: 32 (over x_hi, z), tensor: 16 (over x_lo, y, core).
Axes of the slice: x: 4 (x_hi: 2, x_lo: 2; x = x_hi * 2 + x_lo), y: 4, z: 16, core: 2. Of those that a mesh axis runs over, the one named last changes fastest.
Arguments:
- hidden_in: bfloat16 [24576, 16384], P('dp', 'tensor'), may hold values from -6 to 6
- kv_grad: bfloat16 [24576, 2048], P('dp', 'tensor'), may hold values from -6 to 6
- frozen_kv: bfloat16 [16384, 2048], P('tensor', 'dp'), may hold values from -0.046875 to 0.046875
- adapter_down: bfloat16 [16384, 64], P('tensor'), may hold values from -0.046875 to 0.046875
- adapter_up: bfloat16 [64, 2048], replicated, may hold values from -0.75 to 0.75
- lengths: int32 [64], P('dp'), may hold values from 1 to 384, 12288 in all
Outputs:
- input_grad: bfloat16 [24576, 16384], P('dp', 'tensor')
- down_grad: float32 [16384, 64], P('tensor')
- up_grad: float32 [64, 2048], P(None, 'tensor')
The draws below stay inside these ranges and needn't reach their ends.
Inputs may be any that keep to these rules, and one draw needn't show every extreme that they name: lengths of the 64 sequences; the longest fills all 384 slots.
All inputs are finite; a program needn't handle non-finite values. No bound on the sum of `lengths` on one device may be relied on, other than what follows from the above.
Results may differ from the reference program's by a relative error of at most 0.0033.
Values may be sent and summed in bfloat16 or wider, within the bound.
No kernel may reach another device: no remote copies, remote signals or barrier semaphores. Data moves between devices by JAX's collectives and lax.ppermute only.
A program may use at most 64 MiB of HBM per device.

```python
import math
import jax
import jax.numpy as jnp
import numpy as np
from jax import lax

D = 16384
KVW = 2048
RANK = 64
SLOTS = 384
SEQS = 64
TOKENS = 24576


def levels(key, extent, pieces, smallest, top_value):
    factor_of = 1.0
    for dim, blocks in pieces:
        draws = jax.random.uniform(jax.random.fold_in(jax.random.fold_in(key, 6), dim), (blocks,), jnp.float32, smallest / len(pieces), top_value / len(pieces))
        factor_of = factor_of * jnp.repeat(jnp.exp(draws), extent[dim] // blocks).reshape((-1,) + (1,) * (len(extent) - 1 - dim))
    return factor_of


def length_profile(count, total, bound, lean):
    weights = [(1 << 20) // math.isqrt(standing ** lean) + 1 for standing in range(2, count + 1)]
    spare, given = total - bound - (count - 1), [1] * (count - 1)
    while spare > 0:
        free = [i for i in range(count - 1) if given[i] < bound]
        pool, remaining = sum([weights[i] for i in free]), spare
        for i in free:
            extra = min(bound - given[i], max(1, remaining * weights[i] // pool), spare)
            given[i] = given[i] + extra
            spare = spare - extra
    return np.array([bound] + given)


def ragged(own_key, number_of, total, reach, slope):
    if number_of == 2:
        one = jax.random.randint(own_key, (), max(1, total - reach), min(reach, total - 1) + 1)
        return jnp.stack([one, total - one])
    sizes = jnp.asarray(length_profile(number_of, total, reach, slope), jnp.int32)
    pairs = (number_of - 1) // 2
    source_of, sink = sizes[1:1 + 2 * pairs:2], sizes[2:2 + 2 * pairs:2]
    slack = jnp.minimum(source_of - 1, reach - sink)
    shifted = jax.random.randint(jax.random.fold_in(own_key, 1), (pairs,), 0, 1 << 20) % (slack + 1)
    sizes = sizes.at[1:1 + 2 * pairs:2].set(source_of - shifted).at[2:2 + 2 * pairs:2].set(sink + shifted)
    return sizes[jax.random.permutation(jax.random.fold_in(own_key, 2), number_of)]


def scatter_about(rng, shape, deviation, most, pieces=(), held_as=jnp.bfloat16):
    drawn = jax.random.normal(rng, shape, jnp.float32) * deviation
    if len(pieces) > 0:
        drawn = levels(rng, shape, pieces, -0.22, 0.18) * drawn
    return jnp.clip(drawn, min=-most, max=most).astype(held_as)


def setup_inputs(seed: int = 0) -> dict:
    arg_keys = jax.random.split(jax.random.key(seed), 7)
    return {
        "hidden_in": scatter_about(arg_keys[0], (TOKENS, D), 1.0, 6.0, ((0, 32), (1, 16))),
        "kv_grad": scatter_about(arg_keys[1], (TOKENS, KVW), 1.0, 6.0, ((0, 32), (1, 16))),
        "frozen_kv": scatter_about(arg_keys[2], (D, KVW), D ** -0.5, 0.046875, ((0, 16), (1, 32))),
        "adapter_down": scatter_about(arg_keys[3], (D, RANK), D ** -0.5, 0.046875, ((0, 16),)),
        "adapter_up": scatter_about(arg_keys[4], (RANK, KVW), RANK ** -0.5, 0.75),
        "lengths": ragged(arg_keys[5], SEQS, SEQS * SLOTS // 2, SLOTS, 2).astype(jnp.int32),
    }


def reference(hidden_in, kv_grad, frozen_kv, adapter_down, adapter_up, lengths):
    position = jnp.arange(TOKENS, dtype=jnp.int32) % SLOTS
    sequence = jnp.arange(TOKENS, dtype=jnp.int32) // SLOTS
    live = position < lengths[sequence]
    masked = jnp.where(live[:, None], kv_grad, jnp.zeros_like(kv_grad)).astype(jnp.bfloat16)
    projected = jnp.dot(hidden_in, adapter_down, preferred_element_type=jnp.float32).astype(jnp.bfloat16)
    coupled = (0.25 * jnp.dot(masked, adapter_up.T, preferred_element_type=jnp.float32)).astype(jnp.bfloat16)
    masked_seq = masked.reshape(SEQS, SLOTS, KVW)
    coupled_seq = coupled.reshape(SEQS, SLOTS, RANK)

    def one_sequence(pair):
        grad_rows, low_rows = pair
        total = jnp.dot(grad_rows, frozen_kv.T, preferred_element_type=jnp.float32)
        total = total + jnp.dot(low_rows, adapter_down.T, preferred_element_type=jnp.float32)
        return total.astype(jnp.bfloat16)

    input_grad = lax.map(one_sequence, (masked_seq, coupled_seq)).reshape(TOKENS, D)
    down_grad = lax.dot_general(hidden_in, coupled, (((0,), (0,)), ((), ())), preferred_element_type=jnp.float32) / SEQS
    up_grad = 0.25 * lax.dot_general(projected, masked, (((0,), (0,)), ((), ())), preferred_element_type=jnp.float32) / SEQS
    return input_grad, down_grad, up_grad
```

```python
import jax
import jax.numpy as jnp
from jax import lax
from jax.experimental import pallas as pl
from jax.experimental.pallas import tpu as pltpu
from jax.sharding import PartitionSpec as P

NX, NZ = 2, 16
NY, NC = 4, 2
XH_SWAP = [(i, (i + NZ) % (NX * NZ)) for i in range(NX * NZ)]
XH_GROUPS = [[z, z + NZ] for z in range(NZ)]
Z_GROUPS = [[h * NZ + z for z in range(NZ)] for h in range(NX)]
XL_GROUPS = [[i, i + NY * NC] for i in range(NY * NC)]
CORE_SWAP = [(i, i ^ 1) for i in range(2 * NY * NC)]


def y_shift(k):
    return [
        (a * 8 + y * 2 + c, a * 8 + (y + k) % NY * 2 + c)
        for a in range(2)
        for y in range(NY)
        for c in range(NC)
    ]


def dot(left, right, left_dim, right_dim):
    return lax.dot_general(
        left,
        right,
        (((left_dim,), (right_dim,)), ((), ())),
        preferred_element_type=jnp.float32,
    )


def grad_kernel(place, *refs):
    own, other = refs[0:NY], refs[NY : 2 * NY]
    w_ref, low_ref, down_ref, out_ref = refs[2 * NY :]
    y, core = place[0], place[1]
    left, right = [], []
    for r in range(NY):
        source = (y + (NY - r)) % NY
        for a in range(2):
            for side, c in ((own, core), (other, 1 - core)):
                left.append(side[r][a])
                block = w_ref[pl.ds(source * 4 + c * 2, 2), a]
                right.append(block.reshape(128, block.shape[-1]))
    total = jnp.dot(
        jnp.concatenate(left, axis=1),
        jnp.concatenate(right, axis=0),
        preferred_element_type=jnp.float32,
    )
    total += jnp.dot(low_ref[...], down_ref[...], preferred_element_type=jnp.float32)
    out_ref[...] = total.astype(out_ref.dtype)


def input_gradient(place, own, other, w_all, coupled, down_t):
    rows, features, tile = coupled.shape[0], down_t.shape[1], 256
    whole = pl.BlockSpec((2, rows, 128), lambda i, place: (0, 0, 0))
    return pl.pallas_call(
        grad_kernel,
        grid_spec=pltpu.PrefetchScalarGridSpec(
            num_scalar_prefetch=1,
            grid=(features // tile,),
            in_specs=[whole] * (2 * NY)
            + [
                pl.BlockSpec((NZ, NX, 64, tile), lambda i, place: (0, 0, 0, i)),
                pl.BlockSpec((rows, 64), lambda i, place: (0, 0)),
                pl.BlockSpec((64, tile), lambda i, place: (0, i)),
            ],
            out_specs=pl.BlockSpec((rows, tile), lambda i, place: (0, i)),
        ),
        out_shape=jax.ShapeDtypeStruct((rows, features), jnp.bfloat16),
        compiler_params=pltpu.CompilerParams(vmem_limit_bytes=40 * 1024 * 1024),
        cost_estimate=pl.CostEstimate(
            flops=2 * rows * features * 2112, bytes_accessed=9 << 20, transcendentals=0
        ),
    )(place, *own, *other, w_all, coupled, down_t)


def per_device(hidden_in, kv_grad, frozen_kv, adapter_down, adapter_up, lengths):
    rows = hidden_in.shape[0]
    local_seqs = lengths.shape[0]
    slots = rows // local_seqs
    total_seqs = local_seqs * lax.axis_size("dp")
    members = lax.axis_size("tensor")
    me = lax.axis_index("tensor")
    place = jnp.stack([me // 2 % NY, me % 2]).astype(jnp.int32)

    w_pair = lax.all_gather(frozen_kv.T, "dp", axis=0, axis_index_groups=XH_GROUPS)
    w_all = lax.all_gather(w_pair, "dp", axis=0, axis_index_groups=Z_GROUPS)

    position = jnp.arange(slots, dtype=jnp.int32)
    live = (position[None, :] < lengths[:, None]).reshape(rows, 1)
    masked = jnp.where(live, kv_grad, jnp.zeros_like(kv_grad))

    up_mine = lax.dynamic_slice_in_dim(adapter_up, me * 128, 128, axis=1)
    parts = jnp.concatenate(
        [dot(hidden_in, adapter_down, 1, 0), 0.25 * dot(masked, up_mine, 1, 1)], axis=1
    )
    parts = parts.reshape(members, rows // members, 128)
    summed = lax.all_to_all(parts, "tensor", 0, 0).sum(axis=0).astype(jnp.bfloat16)
    spread = jnp.broadcast_to(summed[None], (members,) + summed.shape)
    low_rows = lax.all_to_all(spread, "tensor", 0, 0).reshape(rows, 128)
    projected, coupled = low_rows[:, :64], low_rows[:, 64:]

    down_part = dot(coupled, hidden_in, 0, 0) / total_seqs
    up_part = 0.25 / total_seqs * dot(projected, masked, 0, 0)
    grads = jnp.concatenate([down_part, up_part], axis=1)
    grads = grads.reshape(NZ, 64 // NZ, grads.shape[1])
    share = lax.all_to_all(grads, "dp", 0, 0, axis_index_groups=Z_GROUPS).sum(axis=0)
    share = share + lax.ppermute(share, "dp", XH_SWAP)
    spread = jnp.broadcast_to(share[None], (NZ,) + share.shape)
    grads = lax.all_to_all(spread, "dp", 0, 0, axis_index_groups=Z_GROUPS)
    grads = grads.reshape(64, grads.shape[2])
    down_grad, up_grad = grads[:, : hidden_in.shape[1]].T, grads[:, hidden_in.shape[1] :]

    pair = lax.all_gather(masked, "tensor", axis=0, axis_index_groups=XL_GROUPS)
    own = [pair] + [lax.ppermute(pair, "tensor", y_shift(r)) for r in range(1, NY)]
    other = [lax.ppermute(block, "tensor", CORE_SWAP) for block in own]

    input_grad = input_gradient(place, own, other, w_all, coupled, adapter_down.T)
    return input_grad, down_grad, up_grad


def solution(mesh):
    in_specs = (
        P("dp", "tensor"),
        P("dp", "tensor"),
        P("tensor", "dp"),
        P("tensor", None),
        P(),
        P("dp"),
    )
    out_specs = (P("dp", "tensor"), P("tensor", None), P(None, "tensor"))
    return jax.shard_map(
        per_device, mesh=mesh, in_specs=in_specs, out_specs=out_specs, check_vma=False
    )
```

```python
import jax
import jax.numpy as jnp
from jax import lax
from jax.experimental import pallas as pl
from jax.experimental.pallas import tpu as pltpu
from jax.sharding import PartitionSpec as P

NX, NZ = 2, 16
NT = 16
NY, NC = 4, 2
XH_SWAP = [(i, (i + NZ) % (NX * NZ)) for i in range(NX * NZ)]
XH_GROUPS = [[z, z + NZ] for z in range(NZ)]
Z_GROUPS = [[h * NZ + z for z in range(NZ)] for h in range(NX)]
XL_SWAP = [(i, i ^ (NY * NC)) for i in range(2 * NY * NC)]
CORE_SWAP = [(i, i ^ 1) for i in range(2 * NY * NC)]


def y_shift(k):
    return [
        (a * 8 + y * 2 + c, a * 8 + (y + k) % NY * 2 + c)
        for a in range(2)
        for y in range(NY)
        for c in range(NC)
    ]


def dot(left, right, left_dim, right_dim):
    return lax.dot_general(
        left,
        right,
        (((left_dim,), (right_dim,)), ((), ())),
        preferred_element_type=jnp.float32,
    )


def grad_kernel(place, *refs):
    own, other = refs[:NY], refs[NY : 2 * NY]
    low_ref, w_hbm, down_ref, out_ref, w_ref, total, sems = refs[2 * NY :]
    x_lo, y, core = place[0], place[1], place[2]
    copies = []
    for r in range(NY):
        source = (y + (NY - r)) % NY * 4
        for k in range(4):
            half = x_lo if k < 2 else 1 - x_lo
            column = core if k % 2 == 0 else 1 - core
            copies.append(
                pltpu.make_async_copy(
                    w_hbm.at[pl.ds(source + column * 2, 2), half],
                    w_ref.at[r, k],
                    sems.at[r * 4 + k],
                )
            )
            copies[-1].start()
    total[...] = jnp.dot(
        low_ref[:, 64:], down_ref[...], preferred_element_type=jnp.float32
    )
    for r in range(NY):
        for k in range(4):
            copies[r * 4 + k].wait()
        left = [own[r][0], other[r][0], own[r][1], other[r][1]]
        total[...] += jnp.dot(
            jnp.concatenate(left, axis=1),
            w_ref[r].reshape(512, w_ref.shape[-1]),
            preferred_element_type=jnp.float32,
        )
    out_ref[...] = total[...].astype(out_ref.dtype)


def input_gradient(place, own, other, low_rows, w_all, down_t):
    rows, features = low_rows.shape[0], down_t.shape[1]
    vmem = pl.BlockSpec(memory_space=pltpu.VMEM)
    return pl.pallas_call(
        grad_kernel,
        grid_spec=pltpu.PrefetchScalarGridSpec(
            num_scalar_prefetch=1,
            in_specs=[vmem] * (2 * NY + 1) + [pl.BlockSpec(memory_space=pltpu.HBM), vmem],
            out_specs=vmem,
            scratch_shapes=[
                pltpu.VMEM((NY, 4, 2, 64, features), jnp.bfloat16),
                pltpu.VMEM((rows, features), jnp.float32),
                pltpu.SemaphoreType.DMA((4 * NY,)),
            ],
        ),
        out_shape=jax.ShapeDtypeStruct((rows, features), jnp.bfloat16),
        compiler_params=pltpu.CompilerParams(vmem_limit_bytes=58 * 1024 * 1024),
        cost_estimate=pl.CostEstimate(
            flops=2 * rows * features * 2112, bytes_accessed=9 << 20, transcendentals=0
        ),
    )(place, *own, *other, low_rows, w_all, down_t)


def per_device(hidden_in, kv_grad, frozen_kv, adapter_down, adapter_up, lengths):
    rows, features = hidden_in.shape
    local_seqs = lengths.shape[0]
    slots = rows // local_seqs
    total_seqs = local_seqs * lax.axis_size("dp")
    me = lax.axis_index("tensor")
    place = jnp.stack([me // 8, me // 2 % NY, me % 2]).astype(jnp.int32)

    position = jnp.arange(slots, dtype=jnp.int32)
    live = (position[None, :] < lengths[:, None]).reshape(rows, 1)
    masked = jnp.where(live, kv_grad, jnp.zeros_like(kv_grad))

    w_pair = lax.all_gather(frozen_kv.T, "dp", axis=0, axis_index_groups=XH_GROUPS)
    w_all = lax.all_gather(w_pair, "dp", axis=0, axis_index_groups=Z_GROUPS)

    up_mine = lax.dynamic_slice_in_dim(adapter_up, me * 128, 128, axis=1)
    parts = jnp.concatenate(
        [dot(hidden_in, adapter_down, 1, 0), 0.25 * dot(masked, up_mine, 1, 1)], axis=1
    )
    parts = parts.reshape(NT, rows // NT, 128)
    parts, w_pair, to_swap = lax.optimization_barrier((parts, w_pair, masked))
    parts = lax.all_to_all(parts, "tensor", 0, 0)
    swapped = lax.ppermute(to_swap, "tensor", XL_SWAP)
    parts, swapped = lax.optimization_barrier((parts, swapped))
    pair = jnp.stack([masked, swapped])
    summed = parts.sum(axis=0).astype(jnp.bfloat16)
    spread = jnp.broadcast_to(summed[None], (NT,) + summed.shape)
    low_rows = lax.all_to_all(spread, "tensor", 0, 0).reshape(rows, 128)
    low_rows, pair = lax.optimization_barrier((low_rows, pair))
    projected, coupled = low_rows[:, :64], low_rows[:, 64:]

    own = [pair] + [lax.ppermute(pair, "tensor", y_shift(r)) for r in range(1, NY)]
    half = features // 2
    down_part = dot(coupled, hidden_in, 0, 0) / total_seqs
    up_part = 0.25 / total_seqs * dot(projected, masked, 0, 0)
    up_part = jnp.concatenate([up_part, jnp.zeros_like(up_part)], axis=1)
    grads = jnp.concatenate(
        [
            down_part.reshape(8, 8, 2, half).swapaxes(1, 2),
            up_part.reshape(8, 8, 2, 128).swapaxes(1, 2),
        ],
        axis=3,
    )
    grads = grads.reshape(NZ, 8, half + 128).astype(jnp.bfloat16)
    grads = lax.all_to_all(grads, "dp", 0, 0, axis_index_groups=Z_GROUPS)
    other = [lax.ppermute(pair, "tensor", CORE_SWAP)]
    grads, own[1], own[3], other[0] = lax.optimization_barrier(
        (grads, own[1], own[3], other[0])
    )

    share = grads.astype(jnp.float32).sum(axis=0)
    share = share + lax.ppermute(share, "dp", XH_SWAP)
    share, own[2] = lax.optimization_barrier((share, own[2]))
    spread = jnp.broadcast_to(share[None], (NZ,) + share.shape)
    grads = lax.all_to_all(spread, "dp", 0, 0, axis_index_groups=Z_GROUPS)
    other += [lax.ppermute(block, "tensor", CORE_SWAP) for block in own[1:]]
    input_grad = input_gradient(place, own, other, low_rows, w_all, adapter_down.T)
    grads, input_grad = lax.optimization_barrier((grads, input_grad))
    grads = grads.reshape(8, 2, 8, half + 128)
    down_grad = grads[..., :half].swapaxes(1, 2).reshape(64, features).T
    up_grad = grads[:, 0, :, half:].reshape(64, 128)
    return input_grad, down_grad, up_grad


def solution(mesh):
    in_specs = (
        P("dp", "tensor"),
        P("dp", "tensor"),
        P("tensor", "dp"),
        P("tensor", None),
        P(),
        P("dp"),
    )
    out_specs = (P("dp", "tensor"), P("tensor", None), P(None, "tensor"))
    return jax.shard_map(
        per_device, mesh=mesh, in_specs=in_specs, out_specs=out_specs, check_vma=False
    )
```

```python
import jax
import jax.numpy as jnp
from jax import lax
from jax.experimental import pallas as pl
from jax.experimental.pallas import tpu as pltpu
from jax.sharding import PartitionSpec as P

NX, NZ = 2, 16
NT = 16
NY, NC = 4, 2
XH_SWAP = [(i, (i + NZ) % (NX * NZ)) for i in range(NX * NZ)]
XH_GROUPS = [[z, z + NZ] for z in range(NZ)]
Z_GROUPS = [[h * NZ + z for z in range(NZ)] for h in range(NX)]
XL_SWAP = [(i, i ^ (NY * NC)) for i in range(2 * NY * NC)]
CORE_SWAP = [(i, i ^ 1) for i in range(2 * NY * NC)]


def y_shift(k):
    return [
        (a * 8 + y * 2 + c, a * 8 + (y + k) % NY * 2 + c)
        for a in range(2)
        for y in range(NY)
        for c in range(NC)
    ]


def dot(left, right, left_dim, right_dim):
    return lax.dot_general(
        left,
        right,
        (((left_dim,), (right_dim,)), ((), ())),
        preferred_element_type=jnp.float32,
    )


def grad_kernel(place, *refs):
    own, other, refs = refs[:NY], refs[NY : 2 * NY], refs[2 * NY :]
    (low_ref, w_hbm, down_ref, out_hbm), refs = refs[:4], refs[4:]
    g_ref, w_ref, total, out_ref, g_sems, w_sems, out_sems = refs
    x_lo, y, core = place[0], place[1], place[2]
    rows, features = out_ref.shape
    copies = []
    for r in range(NY):
        source = (y + (NY - r)) % NY * 4
        for k in range(4):
            half = x_lo if k < 2 else 1 - x_lo
            column = core if k % 2 == 0 else 1 - core
            part = w_hbm.at[pl.ds(source + column * 2, 2), half]
            at = r * 4 + k
            copies.append(pltpu.make_async_copy(part, w_ref.at[r, k], w_sems.at[at]))
            copies.append(
                pltpu.make_async_copy(
                    (own, other)[k % 2][r].at[k // 2], g_ref.at[r, k], g_sems.at[at]
                )
            )
    for copy in copies:
        copy.start()
    total[...] = jnp.dot(
        low_ref[:, 64:], down_ref[...], preferred_element_type=jnp.float32
    )
    results = []
    for r in range(NY):
        for copy in copies[r * 8 : r * 8 + 8]:
            copy.wait()
        right = w_ref[r].reshape(512, features)
        height = rows if r < NY - 1 else rows // 3
        for i in range(rows // height):
            at = pl.ds(i * height, height)
            left = jnp.concatenate([g_ref[r, k, at, :] for k in range(4)], axis=1)
            sums = total[at, :] + jnp.dot(left, right, preferred_element_type=jnp.float32)
            if r < NY - 1:
                total[at, :] = sums
            else:
                out_ref[at, :] = sums.astype(out_ref.dtype)
                results.append(
                    pltpu.make_async_copy(
                        out_ref.at[at], out_hbm.at[at], out_sems.at[i]
                    )
                )
                results[i].start()
    for copy in results:
        copy.wait()


def input_gradient(place, own, other, low_rows, w_all, down_t):
    rows, features = low_rows.shape[0], down_t.shape[1]
    vmem = pl.BlockSpec(memory_space=pltpu.VMEM)
    hbm = pl.BlockSpec(memory_space=pltpu.HBM)
    return pl.pallas_call(
        grad_kernel,
        grid_spec=pltpu.PrefetchScalarGridSpec(
            num_scalar_prefetch=1,
            in_specs=[hbm] * (2 * NY) + [vmem, hbm, vmem],
            out_specs=hbm,
            scratch_shapes=[
                pltpu.VMEM((NY, 4, rows, 128), jnp.bfloat16),
                pltpu.VMEM((NY, 4, 2, 64, features), jnp.bfloat16),
                pltpu.VMEM((rows, features), jnp.float32),
                pltpu.VMEM((rows, features), jnp.bfloat16),
                pltpu.SemaphoreType.DMA((4 * NY,)),
                pltpu.SemaphoreType.DMA((4 * NY,)),
                pltpu.SemaphoreType.DMA((3,)),
            ],
        ),
        out_shape=jax.ShapeDtypeStruct((rows, features), jnp.bfloat16),
        compiler_params=pltpu.CompilerParams(vmem_limit_bytes=58 * 1024 * 1024),
        cost_estimate=pl.CostEstimate(
            flops=2 * rows * features * 2112, bytes_accessed=9 << 20, transcendentals=0
        ),
    )(place, *own, *other, low_rows, w_all, down_t)


def per_device(hidden_in, kv_grad, frozen_kv, adapter_down, adapter_up, lengths):
    rows, features = hidden_in.shape
    local_seqs = lengths.shape[0]
    slots = rows // local_seqs
    total_seqs = local_seqs * lax.axis_size("dp")
    me = lax.axis_index("tensor")
    place = jnp.stack([me // 8, me // 2 % NY, me % 2]).astype(jnp.int32)

    w_pair = lax.all_gather(frozen_kv.T, "dp", axis=0, axis_index_groups=XH_GROUPS)
    w_all = lax.all_gather(w_pair, "dp", axis=0, axis_index_groups=Z_GROUPS)

    position = jnp.arange(slots, dtype=jnp.int32)
    live = (position[None, :] < lengths[:, None]).reshape(rows, 1)
    masked = jnp.where(live, kv_grad, jnp.zeros_like(kv_grad))

    up_mine = lax.dynamic_slice_in_dim(adapter_up, me * 128, 128, axis=1)
    parts = jnp.concatenate(
        [dot(hidden_in, adapter_down, 1, 0), 0.25 * dot(masked, up_mine, 1, 1)], axis=1
    )
    parts = parts.reshape(NT, rows // NT, 128)
    parts, w_pair, to_swap = lax.optimization_barrier((parts, w_pair, masked))
    parts = lax.all_to_all(parts, "tensor", 0, 0)
    swapped = lax.ppermute(to_swap, "tensor", XL_SWAP)
    parts, swapped = lax.optimization_barrier((parts, swapped))
    summed = parts.sum(axis=0).astype(jnp.bfloat16)
    spread = jnp.broadcast_to(summed[None], (NT,) + summed.shape)
    low_rows = lax.all_to_all(spread, "tensor", 0, 0).reshape(rows, 128)
    pair = jnp.stack([masked, swapped])
    low_rows, pair = lax.optimization_barrier((low_rows, pair))
    projected, coupled = low_rows[:, :64], low_rows[:, 64:]

    own = [pair, lax.ppermute(pair, "tensor", y_shift(1)), None]
    own += [lax.ppermute(pair, "tensor", y_shift(-1))]
    own[2] = lax.ppermute(own[1], "tensor", y_shift(1))
    half = features // 2
    down_part = dot(coupled, hidden_in, 0, 0) / total_seqs
    up_part = 0.25 / total_seqs * dot(projected, masked, 0, 0)
    up_part = jnp.concatenate([up_part, jnp.zeros_like(up_part)], axis=1)
    grads = jnp.concatenate(
        [
            down_part.reshape(8, 8, 2, half).swapaxes(1, 2),
            up_part.reshape(8, 8, 2, 128).swapaxes(1, 2),
        ],
        axis=3,
    )
    grads = grads.reshape(NZ, 8, half + 128).astype(jnp.bfloat16)
    grads = lax.all_to_all(grads, "dp", 0, 0, axis_index_groups=Z_GROUPS)
    other = [lax.ppermute(pair, "tensor", CORE_SWAP)]
    grads, own[1], own[3], other[0] = lax.optimization_barrier(
        (grads, own[1], own[3], other[0])
    )

    share = grads.astype(jnp.float32).sum(axis=0)
    share = share + lax.ppermute(share, "dp", XH_SWAP)
    share, own[2] = lax.optimization_barrier((share, own[2]))
    spread = jnp.broadcast_to(share.astype(jnp.bfloat16)[None], (NZ,) + share.shape)
    grads = lax.all_to_all(spread, "dp", 0, 0, axis_index_groups=Z_GROUPS)
    other += [lax.ppermute(block, "tensor", CORE_SWAP) for block in own[1:]]
    input_grad = input_gradient(place, own, other, low_rows, w_all, adapter_down.T)
    grads, input_grad = lax.optimization_barrier((grads, input_grad))
    grads = grads.reshape(8, 2, 8, half + 128).astype(jnp.float32)
    down_grad = grads[..., :half].swapaxes(1, 2).reshape(64, features).T
    up_grad = grads[:, 0, :, half:].reshape(64, 128)
    return input_grad, down_grad, up_grad


def solution(mesh):
    in_specs = (
        P("dp", "tensor"),
        P("dp", "tensor"),
        P("tensor", "dp"),
        P("tensor", None),
        P(),
        P("dp"),
    )
    out_specs = (P("dp", "tensor"), P("tensor", None), P(None, "tensor"))
    return jax.shard_map(
        per_device, mesh=mesh, in_specs=in_specs, out_specs=out_specs, check_vma=False
    )
```

```python
import jax
import jax.numpy as jnp
from jax import lax
from jax.experimental import pallas as pl
from jax.experimental.pallas import tpu as pltpu
from jax.sharding import PartitionSpec as P

NX, NZ = 2, 16
NT = 16
NY, NC = 4, 2
XH_SWAP = [(i, (i + NZ) % (NX * NZ)) for i in range(NX * NZ)]
XH_GROUPS = [[z, z + NZ] for z in range(NZ)]
Z_GROUPS = [[h * NZ + z for z in range(NZ)] for h in range(NX)]
XL_SWAP = [(i, i ^ (NY * NC)) for i in range(2 * NY * NC)]
CORE_SWAP = [(i, i ^ 1) for i in range(2 * NY * NC)]


def y_shift(k):
    return [
        (a * 8 + y * 2 + c, a * 8 + (y + k) % NY * 2 + c)
        for a in range(2)
        for y in range(NY)
        for c in range(NC)
    ]


def dot(left, right, left_dim, right_dim):
    return lax.dot_general(
        left,
        right,
        (((left_dim,), (right_dim,)), ((), ())),
        preferred_element_type=jnp.float32,
    )


def grad_kernel(place, *refs):
    blocks, refs = refs[:NY], refs[NY:]
    (low_ref, w_hbm, down_ref, out_hbm), refs = refs[:4], refs[4:]
    g_ref, w_ref, total, out_ref, g_sems, w_sems, out_sems = refs
    x_lo, y, core = place[0], place[1], place[2]
    rows, features = out_ref.shape
    copies = []
    for r in range(NY):
        source = (y + (NY - r)) % NY * 4
        for k in range(4):
            half = x_lo if k < 2 else 1 - x_lo
            column = core if k % 2 == 0 else 1 - core
            part = w_hbm.at[pl.ds(source + column * 2, 2), half]
            at = r * 4 + k
            copies.append(pltpu.make_async_copy(part, w_ref.at[r, k], w_sems.at[at]))
            copies.append(
                pltpu.make_async_copy(
                    blocks[r].at[k % 2, k // 2], g_ref.at[r, k], g_sems.at[at]
                )
            )
    for copy in copies:
        copy.start()
    total[...] = jnp.dot(
        low_ref[:, 64:], down_ref[...], preferred_element_type=jnp.float32
    )
    results = []
    for r in range(NY):
        for copy in copies[r * 8 : r * 8 + 8]:
            copy.wait()
        right = w_ref[r].reshape(512, features)
        height = rows if r < NY - 1 else rows // 3
        for i in range(rows // height):
            at = pl.ds(i * height, height)
            left = jnp.concatenate([g_ref[r, k, at, :] for k in range(4)], axis=1)
            sums = total[at, :] + jnp.dot(left, right, preferred_element_type=jnp.float32)
            if r < NY - 1:
                total[at, :] = sums
            else:
                out_ref[at, :] = sums.astype(out_ref.dtype)
                results.append(
                    pltpu.make_async_copy(
                        out_ref.at[at], out_hbm.at[at], out_sems.at[i]
                    )
                )
                results[i].start()
    for copy in results:
        copy.wait()


def input_gradient(place, blocks, low_rows, w_all, down_t):
    rows, features = low_rows.shape[0], down_t.shape[1]
    vmem = pl.BlockSpec(memory_space=pltpu.VMEM)
    hbm = pl.BlockSpec(memory_space=pltpu.HBM)
    return pl.pallas_call(
        grad_kernel,
        grid_spec=pltpu.PrefetchScalarGridSpec(
            num_scalar_prefetch=1,
            in_specs=[hbm] * NY + [vmem, hbm, vmem],
            out_specs=hbm,
            scratch_shapes=[
                pltpu.VMEM((NY, 4, rows, 128), jnp.bfloat16),
                pltpu.VMEM((NY, 4, 2, 64, features), jnp.bfloat16),
                pltpu.VMEM((rows, features), jnp.float32),
                pltpu.VMEM((rows, features), jnp.bfloat16),
                pltpu.SemaphoreType.DMA((4 * NY,)),
                pltpu.SemaphoreType.DMA((4 * NY,)),
                pltpu.SemaphoreType.DMA((3,)),
            ],
        ),
        out_shape=jax.ShapeDtypeStruct((rows, features), jnp.bfloat16),
        compiler_params=pltpu.CompilerParams(vmem_limit_bytes=58 * 1024 * 1024),
        cost_estimate=pl.CostEstimate(
            flops=2 * rows * features * 2112, bytes_accessed=9 << 20, transcendentals=0
        ),
    )(place, *blocks, low_rows, w_all, down_t)


def per_device(hidden_in, kv_grad, frozen_kv, adapter_down, adapter_up, lengths):
    rows, features = hidden_in.shape
    local_seqs = lengths.shape[0]
    slots = rows // local_seqs
    total_seqs = local_seqs * lax.axis_size("dp")
    me = lax.axis_index("tensor")
    place = jnp.stack([me // 8, me // 2 % NY, me % 2]).astype(jnp.int32)

    w_pair = lax.all_gather(frozen_kv.T, "dp", axis=0, axis_index_groups=XH_GROUPS)
    w_all = lax.all_gather(w_pair, "dp", axis=0, axis_index_groups=Z_GROUPS)

    position = jnp.arange(slots, dtype=jnp.int32)
    live = (position[None, :] < lengths[:, None]).reshape(rows, 1)
    masked = jnp.where(live, kv_grad, jnp.zeros_like(kv_grad))

    up_mine = lax.dynamic_slice_in_dim(adapter_up, me * 128, 128, axis=1)
    parts = jnp.concatenate(
        [dot(hidden_in, adapter_down, 1, 0), 0.25 * dot(masked, up_mine, 1, 1)], axis=1
    )
    parts = parts.reshape(NT, rows // NT, 128)
    parts, w_pair, to_swap = lax.optimization_barrier((parts, w_pair, masked))
    parts = lax.all_to_all(parts, "tensor", 0, 0)
    swapped = lax.ppermute(to_swap, "tensor", XL_SWAP)
    parts, swapped = lax.optimization_barrier((parts, swapped))
    summed = parts.sum(axis=0).astype(jnp.bfloat16)
    spread = jnp.broadcast_to(summed[None], (NT,) + summed.shape)
    pair = jnp.stack([masked, swapped])
    spread, pair = lax.optimization_barrier((spread, pair))
    low_rows = lax.all_to_all(spread, "tensor", 0, 0).reshape(rows, 128)
    pair_other = lax.ppermute(pair, "tensor", CORE_SWAP)
    low_rows, pair_other = lax.optimization_barrier((low_rows, pair_other))
    projected, coupled = low_rows[:, :64], low_rows[:, 64:]

    half = features // 2
    down_part = dot(coupled, hidden_in, 0, 0) / total_seqs
    up_part = 0.25 / total_seqs * dot(projected, masked, 0, 0)
    up_part = jnp.pad(up_part, ((0, 0), (0, 128)))
    grads = jnp.concatenate(
        [
            down_part.reshape(8, 8, 2, half).swapaxes(1, 2),
            up_part.reshape(8, 8, 2, 128).swapaxes(1, 2),
        ],
        axis=3,
    )
    grads = grads.reshape(NZ, 8, half + 128).astype(jnp.bfloat16)
    grads, pair, pair_other = lax.optimization_barrier((grads, pair, pair_other))
    grads = lax.all_to_all(grads, "dp", 0, 0, axis_index_groups=Z_GROUPS)
    block = jnp.stack([pair, pair_other])
    blocks = [block, lax.ppermute(block, "tensor", y_shift(1)), None]
    blocks += [lax.ppermute(block, "tensor", y_shift(-1))]
    blocks[2] = lax.ppermute(blocks[1], "tensor", y_shift(1))
    grads, blocks[1] = lax.optimization_barrier((grads, blocks[1]))

    share = grads.astype(jnp.float32).sum(axis=0)
    share = share + lax.ppermute(share, "dp", XH_SWAP)
    share, blocks[3] = lax.optimization_barrier((share, blocks[3]))
    spread = jnp.broadcast_to(share.astype(jnp.bfloat16)[None], (NZ,) + share.shape)
    grads = lax.all_to_all(spread, "dp", 0, 0, axis_index_groups=Z_GROUPS)
    input_grad = input_gradient(place, blocks, low_rows, w_all, adapter_down.T)
    grads, input_grad = lax.optimization_barrier((grads, input_grad))
    grads = grads.reshape(8, 2, 8, half + 128).astype(jnp.float32)
    down_grad = grads[..., :half].swapaxes(1, 2).reshape(64, features).T
    up_grad = grads[:, 0, :, half:].reshape(64, 128)
    return input_grad, down_grad, up_grad


def solution(mesh):
    in_specs = (
        P("dp", "tensor"),
        P("dp", "tensor"),
        P("tensor", "dp"),
        P("tensor", None),
        P(),
        P("dp"),
    )
    out_specs = (P("dp", "tensor"), P("tensor", None), P(None, "tensor"))
    return jax.shard_map(
        per_device, mesh=mesh, in_specs=in_specs, out_specs=out_specs, check_vma=False
    )
```

```python
import jax
import jax.numpy as jnp
from jax import lax
from jax.experimental import pallas as pl
from jax.experimental.pallas import tpu as pltpu
from jax.sharding import PartitionSpec as P

NX, NZ = 2, 16
NT = 16
NY, NC = 4, 2
XH_SWAP = [(i, (i + NZ) % (NX * NZ)) for i in range(NX * NZ)]
XH_GROUPS = [[z, z + NZ] for z in range(NZ)]
Z_GROUPS = [[h * NZ + z for z in range(NZ)] for h in range(NX)]
XL_SWAP = [(i, i ^ (NY * NC)) for i in range(2 * NY * NC)]
CORE_SWAP = [(i, i ^ 1) for i in range(2 * NY * NC)]


def y_shift(k):
    return [
        (a * 8 + y * 2 + c, a * 8 + (y + k) % NY * 2 + c)
        for a in range(2)
        for y in range(NY)
        for c in range(NC)
    ]


def dot(left, right, left_dim, right_dim):
    return lax.dot_general(
        left,
        right,
        (((left_dim,), (right_dim,)), ((), ())),
        preferred_element_type=jnp.float32,
    )


def grad_kernel(place, *refs):
    blocks, refs = refs[:NY], refs[NY:]
    (low_ref, w_hbm, down_ref, out_hbm), refs = refs[:4], refs[4:]
    g_ref, w_ref, total, out_ref, g_sems, w_sems, out_sems = refs
    x_lo, y, core = place[0], place[1], place[2]
    rows, features = out_ref.shape
    copies = []
    for r in range(NY):
        source = (y + (NY - r)) % NY * 4
        for k in range(4):
            half = x_lo if k < 2 else 1 - x_lo
            column = core if k % 2 == 0 else 1 - core
            part = w_hbm.at[pl.ds(source + column * 2, 2), half]
            at = r * 4 + k
            copies.append(pltpu.make_async_copy(part, w_ref.at[r, k], w_sems.at[at]))
            copies.append(
                pltpu.make_async_copy(
                    blocks[r].at[k // 2, k % 2], g_ref.at[r, k], g_sems.at[at]
                )
            )
    for copy in copies:
        copy.start()
    total[...] = jnp.dot(
        low_ref[:, 64:], down_ref[...], preferred_element_type=jnp.float32
    )
    results = []
    for r in range(NY):
        for copy in copies[r * 8 : r * 8 + 8]:
            copy.wait()
        right = w_ref[r].reshape(512, features)
        height = rows if r < NY - 1 else rows // 3
        for i in range(rows // height):
            at = pl.ds(i * height, height)
            left = jnp.concatenate([g_ref[r, k, at, :] for k in range(4)], axis=1)
            sums = total[at, :] + jnp.dot(left, right, preferred_element_type=jnp.float32)
            if r < NY - 1:
                total[at, :] = sums
            else:
                out_ref[at, :] = sums.astype(out_ref.dtype)
                results.append(
                    pltpu.make_async_copy(
                        out_ref.at[at], out_hbm.at[at], out_sems.at[i]
                    )
                )
                results[i].start()
    for copy in results:
        copy.wait()


def input_gradient(place, blocks, low_rows, w_all, down_t):
    rows, features = low_rows.shape[0], down_t.shape[1]
    vmem = pl.BlockSpec(memory_space=pltpu.VMEM)
    hbm = pl.BlockSpec(memory_space=pltpu.HBM)
    return pl.pallas_call(
        grad_kernel,
        grid_spec=pltpu.PrefetchScalarGridSpec(
            num_scalar_prefetch=1,
            in_specs=[hbm] * NY + [vmem, hbm, vmem],
            out_specs=hbm,
            scratch_shapes=[
                pltpu.VMEM((NY, 4, rows, 128), jnp.bfloat16),
                pltpu.VMEM((NY, 4, 2, 64, features), jnp.bfloat16),
                pltpu.VMEM((rows, features), jnp.float32),
                pltpu.VMEM((rows, features), jnp.bfloat16),
                pltpu.SemaphoreType.DMA((4 * NY,)),
                pltpu.SemaphoreType.DMA((4 * NY,)),
                pltpu.SemaphoreType.DMA((3,)),
            ],
        ),
        out_shape=jax.ShapeDtypeStruct((rows, features), jnp.bfloat16),
        compiler_params=pltpu.CompilerParams(vmem_limit_bytes=58 * 1024 * 1024),
        cost_estimate=pl.CostEstimate(
            flops=2 * rows * features * 2112, bytes_accessed=9 << 20, transcendentals=0
        ),
    )(place, *blocks, low_rows, w_all, down_t)


def parts_kernel(lengths, me, hidden, kv_grad, down_t, up, masked, parts):
    rows, slots = kv_grad.shape[0], kv_grad.shape[0] // lengths.shape[0]
    for i in range(lengths.shape[0]):
        at = pl.ds(i * slots, slots)
        position = lax.broadcasted_iota(jnp.int32, (slots, 128), 0)
        mine = jnp.where(position < lengths[i], kv_grad[at, :].astype(jnp.float32), 0.0)
        masked[at, :] = mine.astype(masked.dtype)
    up_mine = up[:, pl.ds(pl.multiple_of(me[0] * 128, 128), 128)]
    both = jnp.concatenate(
        [dot(hidden[...], down_t[...], 1, 1), 0.25 * dot(masked[...], up_mine, 1, 1)],
        axis=1,
    )
    parts[...] = both.reshape(parts.shape)


def low_parts(lengths, me, hidden, kv_grad, down_t, up):
    rows = kv_grad.shape[0]
    smem = pl.BlockSpec(memory_space=pltpu.SMEM)
    whole = lambda a: pl.BlockSpec(a.shape, lambda i: (0,) * len(a.shape))
    out_shape = (
        jax.ShapeDtypeStruct((rows, 128), jnp.bfloat16),
        jax.ShapeDtypeStruct((NT, rows // NT, 128), jnp.float32),
    )
    return pl.pallas_call(
        parts_kernel,
        grid=(1,),
        in_specs=[smem, smem] + [whole(a) for a in (hidden, kv_grad, down_t, up)],
        out_specs=tuple(whole(a) for a in out_shape),
        out_shape=out_shape,
        compiler_params=pltpu.CompilerParams(vmem_limit_bytes=58 * 1024 * 1024),
    )(lengths, me, hidden, kv_grad, down_t, up)


def per_device(hidden_in, kv_grad, frozen_kv, adapter_down, adapter_up, lengths):
    rows, features = hidden_in.shape
    local_seqs = lengths.shape[0]
    total_seqs = local_seqs * lax.axis_size("dp")
    me = lax.axis_index("tensor")
    place = jnp.stack([me // 8, me // 2 % NY, me % 2]).astype(jnp.int32)

    w_pair = lax.all_gather(frozen_kv.T, "dp", axis=0, axis_index_groups=XH_GROUPS)
    w_all = lax.all_gather(w_pair, "dp", axis=0, axis_index_groups=Z_GROUPS)

    masked, parts = low_parts(
        lengths, me.astype(jnp.int32).reshape(1), hidden_in, kv_grad, adapter_down.T, adapter_up
    )
    parts, w_pair, to_swap = lax.optimization_barrier((parts, w_pair, masked))
    parts = lax.all_to_all(parts, "tensor", 0, 0)
    swapped = lax.ppermute(to_swap, "tensor", CORE_SWAP)
    parts, swapped = lax.optimization_barrier((parts, swapped))
    summed = parts.sum(axis=0).astype(jnp.bfloat16)
    spread = jnp.broadcast_to(summed[None], (NT,) + summed.shape)
    pair = jnp.stack([masked, swapped])
    spread, pair = lax.optimization_barrier((spread, pair))
    low_rows = lax.all_to_all(spread, "tensor", 0, 0).reshape(rows, 128)
    pair_other = lax.ppermute(pair, "tensor", XL_SWAP)
    low_rows, pair_other = lax.optimization_barrier((low_rows, pair_other))
    projected, coupled = low_rows[:, :64], low_rows[:, 64:]

    half = features // 2
    down_part = dot(coupled, hidden_in, 0, 0) / total_seqs
    up_part = 0.25 / total_seqs * dot(projected, masked, 0, 0)
    up_part = jnp.pad(up_part, ((0, 0), (0, 128)))
    grads = jnp.concatenate(
        [
            down_part.reshape(8, 8, 2, half).swapaxes(1, 2),
            up_part.reshape(8, 8, 2, 128).swapaxes(1, 2),
        ],
        axis=3,
    )
    grads = grads.reshape(NZ, 8, half + 128).astype(jnp.bfloat16)
    grads, pair, pair_other = lax.optimization_barrier((grads, pair, pair_other))
    grads = lax.all_to_all(grads, "dp", 0, 0, axis_index_groups=Z_GROUPS)
    block = jnp.stack([pair, pair_other])
    blocks = [block, lax.ppermute(block, "tensor", y_shift(1)), None]
    blocks += [lax.ppermute(block, "tensor", y_shift(-1))]
    blocks[2] = lax.ppermute(blocks[1], "tensor", y_shift(1))
    grads, blocks[1] = lax.optimization_barrier((grads, blocks[1]))

    share = grads.astype(jnp.float32).sum(axis=0)
    share = share + lax.ppermute(share, "dp", XH_SWAP)
    share, blocks[3] = lax.optimization_barrier((share, blocks[3]))
    spread = jnp.broadcast_to(share.astype(jnp.bfloat16)[None], (NZ,) + share.shape)
    grads = lax.all_to_all(spread, "dp", 0, 0, axis_index_groups=Z_GROUPS)
    input_grad = input_gradient(place, blocks, low_rows, w_all, adapter_down.T)
    grads, input_grad = lax.optimization_barrier((grads, input_grad))
    grads = grads.reshape(8, 2, 8, half + 128).astype(jnp.float32)
    down_grad = grads[..., :half].swapaxes(1, 2).reshape(64, features).T
    up_grad = grads[:, 0, :, half:].reshape(64, 128)
    return input_grad, down_grad, up_grad


def solution(mesh):
    in_specs = (
        P("dp", "tensor"),
        P("dp", "tensor"),
        P("tensor", "dp"),
        P("tensor", None),
        P(),
        P("dp"),
    )
    out_specs = (P("dp", "tensor"), P("tensor", None), P(None, "tensor"))
    return jax.shard_map(
        per_device, mesh=mesh, in_specs=in_specs, out_specs=out_specs, check_vma=False
    )
```
